32 devices in a mesh: dp: 8 (over y, x, core), seq: 4 (over z).
Axes of the slice: x: 2, y: 2, z: 4, core: 2. Of those that a mesh axis runs over, the one named last changes fastest.
Arguments:
- hidden: bfloat16 [8, 512, 4096], P('dp', 'seq'), may hold values from -6 to 6
- head_weight: bfloat16 [16384, 4096], P('seq', 'dp'), may hold values from -0.09375 to 0.09375
- head_bias: bfloat16 [16384], P('seq'), may hold values from -4 to 4
- argmax: int32 [8, 16384], replicated, may hold values from 0 to 512, as said below
- lengths: int32 [8], replicated, may hold values from 128 to 512
- query_terms: bfloat16 [32, 16384], P('dp'), may hold values from 0 to 1
- score_grad: bfloat16 [32, 8], P('dp'), may hold values from -18 to 18
Outputs:
- hidden_grad: bfloat16 [8, 512, 4096], P('dp', 'seq')
The draws below stay inside these ranges and needn't reach their ends.
Inputs may be any that keep to these rules, and one draw needn't show every extreme that they name: `argmax`: every document has exactly 4096 vocabulary entries whose saved position is below 512; all other entries hold 512. For every document, at most 2048 vocabulary entries have their saved position in one aligned block of 128 positions, and in every draw some document reaches 2048 in every block of its first half.
All inputs are finite; a program needn't handle non-finite values.
Results may differ from the reference program's by a relative error of at most 0.005.
Values may be sent and summed in bfloat16 or wider, within the bound.
No kernel may reach another device: no remote copies, remote signals or barrier semaphores. Data moves between devices by JAX's collectives and lax.ppermute only.
A program may use at most 128 MiB of HBM per device.

```python
import jax
import jax.numpy as jnp
from jax import lax

D = 4096
VOC = 16384
TOK_DEV = 128
DOCS = 8
QUERIES = 32
LEN = 512
ACT = 4096


def draw_argmax(key, part):
    key = jax.random.fold_in(key, 17)
    span_key, pick_key, order_key = jax.random.split(key, 3)
    blocks_all = LEN // TOK_DEV
    half_blocks = blocks_all // 2
    spans = jax.random.randint(span_key, (DOCS,), half_blocks, blocks_all + 1)
    chosen = jax.random.randint(pick_key, (), 0, DOCS)
    spans = jnp.where(jnp.arange(DOCS) == chosen, half_blocks, spans)
    extent = spans * TOK_DEV
    orders = jax.vmap(lambda doc_key: jax.random.permutation(doc_key, VOC))(jax.random.split(order_key, DOCS))
    placed = orders * extent[:, None] // ACT
    return jnp.where(orders < ACT, placed, LEN).astype(jnp.int32)


def plant(array, own_key, low, high):
    longest = array.shape.index(max(array.shape))
    spots = []
    for shift in (0, 1):
        where = [jax.random.randint(jax.random.fold_in(own_key, axis), (), 0, length) for axis, length in enumerate(array.shape)]
        where[longest] = (where[longest] + shift) % array.shape[longest]
        spots.append(tuple(where))
    return array.at[spots[0]].set(low).at[spots[1]].set(high)


def level_of(rng, shape, cuts, low, top_value):
    def one(axis_at, blocks):
        heights = jax.random.uniform(jax.random.fold_in(jax.random.fold_in(rng, 6), axis_at), (blocks,), jnp.float32, low / len(cuts), top_value / len(cuts))
        return jnp.repeat(jnp.exp(heights), shape[axis_at] // blocks).reshape((-1,) + (1,) * (len(shape) - axis_at - 1))

    factor_of = one(*cuts[0])
    for cut in cuts[1:]:
        factor_of = factor_of * one(*cut)
    return factor_of


def normal_values(own_key, shape, deviation, limit, cuts=(), held_as=jnp.bfloat16):
    entries = jax.random.normal(own_key, shape, jnp.float32) * deviation
    if len(cuts) > 0:
        entries = level_of(own_key, shape, cuts, -0.22, 0.18) * entries
    return jnp.clip(entries, min=-limit, max=limit).astype(held_as)


def setup_inputs(seed: int = 0) -> dict:
    key_of = jax.random.split(jax.random.key(seed), 8)
    hidden = normal_values(key_of[0], (DOCS, LEN, D), 1.0, 6.0, ((0, 8), (1, 4)))
    head_weight = normal_values(key_of[1], (VOC, D), D ** -0.5, 0.09375, ((0, 4), (1, 8)))
    head_bias = normal_values(key_of[2], (VOC,), 1.0, 4.0, ((0, 4),))
    argmax = draw_argmax(jax.random.fold_in(key_of[7], 71), 0)
    lengths = plant(jax.random.randint(key_of[4], (DOCS,), LEN // 4, LEN + 1), jax.random.fold_in(key_of[4], 1), LEN // 4, LEN).astype(jnp.int32)
    query_terms = jnp.clip(1.0 * jax.random.uniform(key_of[5], (QUERIES, VOC), jnp.float32) ** level_of(key_of[5], (QUERIES, VOC), ((0, 8),), -0.2, 0.2), 0.0, 1.0).astype(jnp.bfloat16)
    score_grad = normal_values(key_of[6], (QUERIES, DOCS), 3.0, 18.0, ((0, 8),))
    return {"hidden": hidden, "head_weight": head_weight, "head_bias": head_bias, "argmax": argmax, "lengths": lengths, "query_terms": query_terms, "score_grad": score_grad}


def reference(hidden, head_weight, head_bias, argmax, lengths, query_terms, score_grad):
    pooled_grad = jnp.dot(score_grad.T, query_terms, preferred_element_type=jnp.float32)
    weight_wide = head_weight.astype(jnp.float32)
    bias_wide = head_bias.astype(jnp.float32)

    def one_document(packed):
        doc_rows, positions, length, grad_row = packed
        clipped = jnp.minimum(positions, doc_rows.shape[0] - 1).astype(jnp.int32)
        picked = doc_rows[clipped].astype(jnp.float32)
        logit_row = jnp.einsum("vk,vk->v", picked, weight_wide, precision=lax.Precision.HIGHEST) + bias_wide
        factor = grad_row * jax.nn.sigmoid(logit_row) / (1.0 + jax.nn.softplus(logit_row))
        pooled_delta = jnp.where(positions < length, factor, jnp.zeros_like(factor)).astype(jnp.bfloat16)
        contrib = pooled_delta.astype(jnp.float32)[:, None] * weight_wide
        hidden_grad = jnp.zeros(doc_rows.shape, jnp.float32).at[clipped].add(contrib)
        return hidden_grad.astype(jnp.bfloat16)

    return lax.map(one_document, (hidden, argmax, lengths, pooled_grad))
```

```python
import functools

import jax
import jax.numpy as jnp
from jax import lax
from jax.experimental import pallas as pl
from jax.experimental.pallas import tpu as pltpu
from jax.sharding import PartitionSpec as P

F32, BF16, I32 = jnp.float32, jnp.bfloat16, jnp.int32
CHUNKS = 2
VMEM_LIMIT = 44 * 1024 * 1024


def tile_of(total, want):
    return want if total % want == 0 else total


def forward_kernel(blocks, tile, place, code, weights, own, *rest):
    from_right, from_left = rest[: blocks - 1], rest[blocks - 1 : 2 * (blocks - 1)]
    out, rows = rest[2 * (blocks - 1) :]
    part = own.shape[1]
    doc = pl.program_id(0)
    rows[pl.ds(0, part), :] = own[0]
    for slot in range(1, blocks):
        where_at = pl.ds(slot * part, part)

        @pl.when(place[0] + slot < blocks)
        def _(slot=slot, where_at=where_at):
            rows[where_at, :] = from_right[slot - 1][0]

        @pl.when(place[0] + slot >= blocks)
        def _(slot=slot, where_at=where_at):
            rows[where_at, :] = from_left[blocks - slot - 1][0]

    held = rows[...]
    for start in range(0, weights.shape[1], tile):
        cols = pl.ds(start, tile)
        scores = jnp.dot(held, weights[:, cols], preferred_element_type=F32)
        ids = lax.broadcasted_iota(I32, scores.shape, 0)
        hit = ids == code[pl.ds(doc, 1), cols]
        out[pl.ds(doc, 1), cols] = jnp.sum(jnp.where(hit, scores, 0.0), axis=0, keepdims=True)


def backward_kernel(blocks, tile, code, weights, logits, pooled, bias, *rest):
    outs, delta = rest[:blocks], rest[blocks]
    part = outs[0].shape[1]
    doc = pl.program_id(0)

    @pl.when(doc == 0)
    def _():
        x = logits[...] + bias[...]
        soft = jnp.maximum(x, 0.0) + jnp.log1p(jnp.exp(-jnp.abs(x)))
        factor = pooled[...] * jax.nn.sigmoid(x) / (1.0 + soft)
        delta[...] = factor.astype(BF16).astype(F32)

    total = jnp.zeros((blocks * part, weights.shape[1]), F32)
    for start in range(0, weights.shape[0], tile):
        cols = pl.ds(start, tile)
        ids = lax.broadcasted_iota(I32, (blocks * part, tile), 0)
        hit = ids == code[pl.ds(doc, 1), cols]
        spread = jnp.where(hit, delta[pl.ds(doc, 1), cols], 0.0).astype(BF16)
        total += jnp.dot(spread, weights[cols, :], preferred_element_type=F32)
    for slot in range(blocks):
        outs[slot][0] = total[slot * part : (slot + 1) * part]


def forward(place, code, weights_t, own, from_right, from_left):
    docs, part, width = own.shape
    blocks = len(from_right) + 1
    entries = weights_t.shape[1]
    rows = pl.BlockSpec((1, part, width), lambda d, s: (d, 0, 0))
    flops = 2 * docs * blocks * part * width * entries
    return pl.pallas_call(
        functools.partial(forward_kernel, blocks, tile_of(entries, 512)),
        out_shape=jax.ShapeDtypeStruct((docs, entries), F32),
        grid_spec=pltpu.PrefetchScalarGridSpec(
            num_scalar_prefetch=1,
            grid=(docs,),
            in_specs=[
                pl.BlockSpec((docs, entries), lambda d, s: (0, 0)),
                pl.BlockSpec((width, entries), lambda d, s: (0, 0)),
            ]
            + [rows] * (2 * blocks - 1),
            out_specs=pl.BlockSpec((docs, entries), lambda d, s: (0, 0)),
            scratch_shapes=[pltpu.VMEM((blocks * part, width), BF16)],
        ),
        compiler_params=pltpu.CompilerParams(vmem_limit_bytes=VMEM_LIMIT),
        cost_estimate=pl.CostEstimate(flops=flops, bytes_accessed=8 << 20, transcendentals=0),
        name="forward",
    )(place, code, weights_t, own, *from_right, *from_left)


def backward(code, weights, logits, pooled, bias, blocks, part):
    docs, entries = code.shape
    width = weights.shape[1]
    whole = pl.BlockSpec((docs, entries), lambda d: (0, 0))
    flops = 2 * docs * blocks * part * width * entries
    return pl.pallas_call(
        functools.partial(backward_kernel, blocks, tile_of(entries, 512)),
        out_shape=[jax.ShapeDtypeStruct((docs, part, width), F32)] * blocks,
        grid=(docs,),
        in_specs=[
            whole,
            pl.BlockSpec((entries, width), lambda d: (0, 0)),
            whole,
            whole,
            pl.BlockSpec((1, entries), lambda d: (0, 0)),
        ],
        out_specs=[pl.BlockSpec((1, part, width), lambda d: (d, 0, 0))] * blocks,
        scratch_shapes=[pltpu.VMEM((docs, entries), F32)],
        compiler_params=pltpu.CompilerParams(vmem_limit_bytes=VMEM_LIMIT),
        cost_estimate=pl.CostEstimate(flops=flops, bytes_accessed=8 << 20, transcendentals=0),
        name="backward",
    )(code, weights, logits, pooled, bias)


def gather_chain(own, blocks):
    from_right, from_left = [], []
    a = b = own
    for hop in range(1, blocks):
        a = lax.ppermute(a, "seq", [(i, i - 1) for i in range(1, blocks - hop + 1)])
        b = lax.ppermute(b, "seq", [(i, i + 1) for i in range(hop - 1, blocks - 1)])
        from_right.append(a)
        from_left.append(b)
    return from_right, from_left


def reduce_chain(grads, blocks):
    up = down = None
    for hop in range(1, blocks):
        a, b = grads[blocks - hop], grads[hop]
        if hop > 1:
            a, b = a + up.astype(F32), b + down.astype(F32)
        up = lax.ppermute(a.astype(BF16), "seq", [(i, i + 1) for i in range(hop)])
        down = lax.ppermute(b.astype(BF16), "seq", [(i, i - 1) for i in range(blocks - hop, blocks)])
    total = grads[0]
    if up is not None:
        total = total + up.astype(F32) + down.astype(F32)
    return total.astype(BF16)


def sum_over_dp(value, size):
    step = 1
    while step < size:
        value = value + lax.ppermute(value, "dp", [(i, i ^ step) for i in range(size)])
        step *= 2
    return value


def on_device(hidden, head_weight, head_bias, argmax, lengths, query_terms, score_grad):
    blocks, size = lax.axis_size("seq"), lax.axis_size("dp")
    z = lax.axis_index("seq")
    tok_rows = hidden.shape[1]
    entries, width = head_weight.shape
    part = tok_rows // CHUNKS

    queries = lax.all_gather(
        lax.dynamic_slice_in_dim(query_terms, z * entries, entries, 1), "dp", axis=0, tiled=True
    )
    score_all = lax.all_gather(score_grad, "dp", axis=0, tiled=True)
    pooled = jnp.einsum("jd,jv->dv", score_all, queries, preferred_element_type=F32)
    bias = head_bias.astype(F32)[None, :]
    weights_t = head_weight.T

    saved = lax.dynamic_slice_in_dim(argmax, z * entries, entries, 1)
    block = saved // tok_rows
    inner = saved - block * tok_rows
    slot = jnp.where(block >= z, block - z, block - z + blocks)
    kept = (block < blocks) & (saved < lengths[:, None])
    place = jnp.reshape(z, (1,)).astype(I32)

    results = []
    for chunk in range(CHUNKS):
        first = chunk * part
        here = kept & (inner >= first) & (inner < first + part)
        code = jnp.where(here, slot * part + inner - first, -1)
        sent = hidden[:, first : first + part]
        sent = sent.reshape(-1, part, size, width).transpose(2, 0, 1, 3).reshape(-1, part, width)
        own = lax.all_to_all(sent, "dp", split_axis=0, concat_axis=0, tiled=True)
        from_right, from_left = gather_chain(own, blocks)
        partial = forward(place, code, weights_t, own, from_right, from_left)
        logits = sum_over_dp(partial, size)
        grads = backward(code, head_weight, logits, pooled, bias, blocks, part)
        mine = reduce_chain(grads, blocks)
        back = lax.all_to_all(mine, "dp", split_axis=0, concat_axis=0, tiled=True)
        back = back.reshape(size, -1, part, width).transpose(1, 2, 0, 3)
        results.append(back.reshape(-1, part, size * width))
    return jnp.concatenate(results, axis=1)


def solution(mesh):
    return jax.shard_map(
        on_device,
        mesh=mesh,
        in_specs=(
            P("dp", "seq", None),
            P("seq", "dp"),
            P("seq"),
            P(),
            P(),
            P("dp", None),
            P("dp", None),
        ),
        out_specs=P("dp", "seq", None),
        check_vma=False,
    )
```

```python
import functools

import jax
import jax.numpy as jnp
from jax import lax
from jax.experimental import pallas as pl
from jax.experimental.pallas import tpu as pltpu
from jax.sharding import PartitionSpec as P

F32, BF16, I32 = jnp.float32, jnp.bfloat16, jnp.int32
SHARES = (4, 4)
VMEM_LIMIT = 28 * 1024 * 1024
TILE = 512
ANY = pl.BlockSpec(memory_space=pl.ANY)


def tile_of(total):
    return TILE if total % TILE == 0 else total


def forward_kernel(slots, grows, code, weights, *rest):
    before, sources, out = rest[:grows], rest[grows : grows + len(slots)], rest[-1]
    codes = code[...]
    total = before[0][...] if grows else jnp.zeros(out.shape, F32)
    for slot, source in zip(slots, sources):
        docs, part, width = source.shape
        rows = source[...].reshape(docs * part, width)
        scores = jnp.dot(rows, weights[...], preferred_element_type=F32)
        scores = scores.reshape(docs, part, scores.shape[1])
        ids = lax.broadcasted_iota(I32, scores.shape, 1) + slot * part
        hit = ids == codes[:, None, :]
        total += jnp.sum(jnp.where(hit, scores, 0.0), axis=1)
    out[...] = total


def backward_kernel(slots, waits, code, weights, logits, pooled, bias, *rest):
    outs = rest[waits:]
    step = pl.program_id(0)
    x = logits[...] + bias[...]
    soft = jnp.maximum(x, 0.0) + jnp.log1p(jnp.exp(-jnp.abs(x)))
    factor = pooled[...] * jax.nn.sigmoid(x) / (1.0 + soft)
    delta = factor.astype(BF16).astype(F32)
    codes = code[...]
    for slot, out in zip(slots, outs):
        docs, part, width = out.shape
        ids = lax.broadcasted_iota(I32, (docs, part, codes.shape[1]), 1) + slot * part
        hit = ids == codes[:, None, :]
        spread = jnp.where(hit, delta[:, None, :], 0.0).astype(BF16)
        spread = spread.reshape(docs * part, codes.shape[1])
        grown = jnp.dot(spread, weights[...], preferred_element_type=F32)
        grown = grown.reshape(docs, part, width)

        @pl.when(step == 0)
        def _():
            out[...] = grown

        @pl.when(step > 0)
        def _():
            out[...] += grown


def forward(code, weights_t, slots, sources, before, waits):
    docs, part, width = sources[0].shape
    entries = weights_t.shape[1]
    tile = tile_of(entries)
    logit = pl.BlockSpec((docs, tile), lambda t: (0, t))
    rows = pl.BlockSpec((docs, part, width), lambda t: (0, 0, 0))
    flops = 2 * docs * part * width * entries * len(slots)
    before = [] if before is None else [before]
    return pl.pallas_call(
        functools.partial(forward_kernel, slots, len(before)),
        out_shape=jax.ShapeDtypeStruct((docs, entries), F32),
        grid=(entries // tile,),
        in_specs=[logit, pl.BlockSpec((width, tile), lambda t: (0, t))]
        + [logit] * len(before)
        + [rows] * len(slots)
        + [ANY] * len(waits),
        out_specs=logit,
        compiler_params=pltpu.CompilerParams(vmem_limit_bytes=VMEM_LIMIT),
        cost_estimate=pl.CostEstimate(flops=flops, bytes_accessed=6 << 20, transcendentals=0),
        name="forward",
    )(code, weights_t, *before, *sources, *waits)


def backward(code, weights, logits, pooled, bias, slots, part, waits):
    docs, entries = code.shape
    width = weights.shape[1]
    tile = tile_of(entries)
    whole = pl.BlockSpec((docs, tile), lambda t: (0, t))
    flops = 2 * docs * part * width * entries * len(slots)
    return pl.pallas_call(
        functools.partial(backward_kernel, slots, len(waits)),
        out_shape=[jax.ShapeDtypeStruct((docs, part, width), F32)] * len(slots),
        grid=(entries // tile,),
        in_specs=[
            whole,
            pl.BlockSpec((tile, width), lambda t: (t, 0)),
            whole,
            whole,
            pl.BlockSpec((1, tile), lambda t: (0, t)),
        ]
        + [ANY] * len(waits),
        out_specs=[pl.BlockSpec((docs, part, width), lambda t: (0, 0, 0))] * len(slots),
        compiler_params=pltpu.CompilerParams(vmem_limit_bytes=VMEM_LIMIT),
        cost_estimate=pl.CostEstimate(flops=flops, bytes_accessed=6 << 20, transcendentals=0),
        name="backward",
    )(code, weights, logits, pooled, bias, *waits)


def together(*values):
    return lax.optimization_barrier(values)


def exchange(value, axis, bit):
    return lax.ppermute(value, axis, [(i, i ^ bit) for i in range(lax.axis_size(axis))])


def on_device(hidden, head_weight, head_bias, argmax, lengths, query_terms, score_grad):
    blocks, size = lax.axis_size("seq"), lax.axis_size("dp")
    z = lax.axis_index("seq")
    tok_rows = hidden.shape[1]
    entries, width = head_weight.shape
    parts = [tok_rows * share // 8 for share in SHARES]
    firsts = [sum(parts[:i]) for i in range(len(parts))]
    count = len(parts)
    near = tuple(range(2, blocks, 2)) + (1,)
    far = tuple(range(3, blocks, 2))
    bits = [1 << i for i in range(blocks.bit_length() - 1)]

    def swap(x):
        return lax.all_to_all(x, "dp", split_axis=0, concat_axis=0, tiled=True)

    sents = []
    for part, first in zip(parts, firsts):
        sent = hidden[:, first : first + part]
        sents.append(sent.reshape(-1, part, size, width).transpose(2, 0, 1, 3).reshape(-1, part, width))

    held = [dict() for _ in range(count)]
    partials, logits = [None] * count, [None] * count
    grads = [dict() for _ in range(count)]
    clock = []

    def tie(*values):
        out = together(*values, *clock)
        clock[:] = out[len(values) :]
        return out[: len(values)]

    def gather_near(c):
        for bit in reversed(bits):
            for slot in sorted(held[c]) if bit > 1 else (0,):
                held[c][slot ^ bit] = exchange(held[c][slot], "seq", bit)

    def gather_far(c):
        for slot in far:
            held[c][slot] = exchange(held[c][slot ^ 1], "seq", 1)

    def run_forward(c, slots, *others):
        sources = [held[c][slot] for slot in slots]
        waits = tuple(clock) + others
        partials[c] = forward(codes[c], weights_t, slots, sources, partials[c], waits)
        clock[:] = [partials[c]]

    def run_backward(c, slots, *others):
        waits = tuple(clock) + others
        found = backward(
            codes[c], head_weight, logits[c], pooled, bias, slots, parts[c], waits
        )
        grads[c].update(zip(slots, found))
        clock[:] = [found[0]]

    def reduce_far(c):
        for slot in reversed(far):
            grads[c][slot] = exchange(grads[c][slot].astype(BF16), "seq", 1)

    def reduce_near(c):
        grads[c][1] = exchange(grads[c][1].astype(BF16), "seq", 1)
        for slot in far:
            grads[c][slot ^ 1] = grads[c][slot ^ 1] + grads[c].pop(slot).astype(F32)
        for bit in bits[1:]:
            for slot in range(blocks - bit, 0, -2 * bit):
                moved = exchange(grads[c].pop(slot).astype(BF16), "seq", bit)
                if slot == bit:
                    grads[c][slot] = moved
                else:
                    grads[c][slot ^ bit] = grads[c][slot ^ bit] + moved.astype(F32)

    def run_sum(value, *between):
        step = 1
        while step < size:
            value = value + exchange(value, "dp", step)
            if between:
                between[0](value)
                between = between[1:]
            step *= 2
        return value

    held[0][0] = swap(sents[0])
    gather_near(0)

    head_weight, saved_all, queries, scores, held[0][0] = together(
        head_weight, argmax, query_terms, score_grad, held[0][0]
    )
    saved = lax.dynamic_slice_in_dim(saved_all, z * entries, entries, 1)
    block = saved // tok_rows
    inner = saved - block * tok_rows
    kept = (block < blocks) & (saved < lengths[:, None])
    codes = []
    for part, first in zip(parts, firsts):
        here = kept & (inner >= first) & (inner < first + part)
        codes.append(jnp.where(here, (block ^ z) * part + inner - first, -1))
    bias = head_bias.astype(F32)[None, :]
    queries = lax.dynamic_slice_in_dim(queries, z * entries, entries, 1)
    pooled = jnp.einsum("jd,jv->dv", scores, queries, preferred_element_type=F32)
    pooled = run_sum(pooled)
    weights_t = head_weight.T
    run_forward(0, (0,))
    for c in range(1, count):
        sents[c], pooled = together(sents[c], pooled)
        held[c][0] = swap(sents[c])
    arrived = [held[0][slot] for slot in near]
    arrived = tie(*arrived, *[held[c][0] for c in range(1, count)])
    held[0].update(zip(near, arrived))
    for c in range(1, count):
        held[c][0] = arrived[len(near) + c - 1]
    gather_far(0)

    for c in range(1, count + 1):
        more = c < count
        if more:
            gather_near(c)
        run_forward(c - 1, near)
        run_forward(c - 1, far, *([grads[c - 2][slot] for slot in far] if c > 1 else ()))
        if c > 1:
            reduce_near(c - 2)
        between = []
        if more:
            between.append(lambda value: run_forward(c, (0,), value))
        elif count > 1:
            between.append(lambda value: run_backward(c - 2, (0,), value))
        logits[c - 1] = run_sum(partials[c - 1], *between)
        if more:
            arrived = tie(*[held[c][slot] for slot in near])
            held[c].update(zip(near, arrived))
            gather_far(c)
        run_backward(c - 1, far)
        reduce_far(c - 1)
        moving = [grads[c - 2][bit] for bit in bits] if c > 1 else ()
        run_backward(c - 1, near, *moving)
    reduce_near(count - 1)
    run_backward(count - 1, (0,))

    results = []
    for c in range(count):
        total = grads[c].pop(0)
        for moved in grads[c].values():
            total = total + moved.astype(F32)
        back = swap(total.astype(BF16))
        back = back.reshape(size, -1, parts[c], width).transpose(1, 2, 0, 3)
        results.append(back.reshape(-1, parts[c], size * width))
    return jnp.concatenate(results, axis=1)


def solution(mesh):
    return jax.shard_map(
        on_device,
        mesh=mesh,
        in_specs=(
            P("dp", "seq", None),
            P("seq", "dp"),
            P("seq"),
            P(),
            P(),
            P("dp", None),
            P("dp", None),
        ),
        out_specs=P("dp", "seq", None),
        check_vma=False,
    )
```

```python
import functools

import jax
import jax.numpy as jnp
from jax import lax
from jax.experimental import pallas as pl
from jax.experimental.pallas import tpu as pltpu
from jax.sharding import PartitionSpec as P

F32, BF16, I32 = jnp.float32, jnp.bfloat16, jnp.int32
SHARES = (4, 4)
VMEM_LIMIT = 28 * 1024 * 1024
TILE = 512
ANY = pl.BlockSpec(memory_space=pl.ANY)


def tile_of(total):
    return TILE if total % TILE == 0 else total


def forward_kernel(slots, grows, joined, code, weights, *rest):
    before, sources, out = rest[:grows], rest[grows : grows + len(slots)], rest[-1]
    codes = code[...]
    total = before[0][...] if grows else jnp.zeros(codes.shape, F32)
    for slot, source in zip(slots, sources):
        docs, part, width = source.shape
        rows = source[...].reshape(docs * part, width)
        scores = jnp.dot(rows, weights[...], preferred_element_type=F32)
        scores = scores.reshape(docs, part, scores.shape[1])
        ids = lax.broadcasted_iota(I32, scores.shape, 1) + slot * part
        hit = ids == codes[:, None, :]
        total += jnp.sum(jnp.where(hit, scores, 0.0), axis=1)
    if joined:
        out[pl.ds(0, codes.shape[0]), :] = total
        out[pl.ds(codes.shape[0], codes.shape[0]), :] = rest[grows + len(slots)][...]
    else:
        out[...] = total


def backward_kernel(slots, waits, code, weights, logits, pooled, bias, *rest):
    outs = rest[waits:]
    step = pl.program_id(0)
    x = logits[...] + bias[...]
    soft = jnp.maximum(x, 0.0) + jnp.log1p(jnp.exp(-jnp.abs(x)))
    factor = pooled[...] * jax.nn.sigmoid(x) / (1.0 + soft)
    delta = factor.astype(BF16).astype(F32)
    codes = code[...]
    for slot, out in zip(slots, outs):
        docs, part, width = out.shape
        ids = lax.broadcasted_iota(I32, (docs, part, codes.shape[1]), 1) + slot * part
        hit = ids == codes[:, None, :]
        spread = jnp.where(hit, delta[:, None, :], 0.0).astype(BF16)
        spread = spread.reshape(docs * part, codes.shape[1])
        grown = jnp.dot(spread, weights[...], preferred_element_type=F32)
        grown = grown.reshape(docs, part, width)

        @pl.when(step == 0)
        def _():
            out[...] = grown

        @pl.when(step > 0)
        def _():
            out[...] += grown


def forward(code, weights_t, slots, sources, before, join, waits):
    docs, part, width = sources[0].shape
    entries = weights_t.shape[1]
    tile = tile_of(entries)
    logit = pl.BlockSpec((docs, tile), lambda t: (0, t))
    rows = pl.BlockSpec((docs, part, width), lambda t: (0, 0, 0))
    flops = 2 * docs * part * width * entries * len(slots)
    before = [] if before is None else [before]
    high = docs * (1 + len(join))
    return pl.pallas_call(
        functools.partial(forward_kernel, slots, len(before), len(join)),
        out_shape=jax.ShapeDtypeStruct((high, entries), F32),
        grid=(entries // tile,),
        in_specs=[logit, pl.BlockSpec((width, tile), lambda t: (0, t))]
        + [logit] * len(before)
        + [rows] * len(slots)
        + [logit] * len(join)
        + [ANY] * len(waits),
        out_specs=pl.BlockSpec((high, tile), lambda t: (0, t)),
        compiler_params=pltpu.CompilerParams(vmem_limit_bytes=VMEM_LIMIT),
        cost_estimate=pl.CostEstimate(flops=flops, bytes_accessed=6 << 20, transcendentals=0),
        name="forward",
    )(code, weights_t, *before, *sources, *join, *waits)


def backward(code, weights, logits, pooled, bias, slots, part, waits):
    docs, entries = code.shape
    width = weights.shape[1]
    tile = tile_of(entries)
    whole = pl.BlockSpec((docs, tile), lambda t: (0, t))
    flops = 2 * docs * part * width * entries * len(slots)
    return pl.pallas_call(
        functools.partial(backward_kernel, slots, len(waits)),
        out_shape=[jax.ShapeDtypeStruct((docs, part, width), F32)] * len(slots),
        grid=(entries // tile,),
        in_specs=[
            whole,
            pl.BlockSpec((tile, width), lambda t: (t, 0)),
            whole,
            pl.BlockSpec((docs, tile), lambda t: (1, t)),
            pl.BlockSpec((1, tile), lambda t: (0, t)),
        ]
        + [ANY] * len(waits),
        out_specs=[pl.BlockSpec((docs, part, width), lambda t: (0, 0, 0))] * len(slots),
        compiler_params=pltpu.CompilerParams(vmem_limit_bytes=VMEM_LIMIT),
        cost_estimate=pl.CostEstimate(flops=flops, bytes_accessed=6 << 20, transcendentals=0),
        name="backward",
    )(code, weights, logits, pooled, bias, *waits)


def together(*values):
    return lax.optimization_barrier(values)


def exchange(value, axis, bit):
    return lax.ppermute(value, axis, [(i, i ^ bit) for i in range(lax.axis_size(axis))])


def on_device(hidden, head_weight, head_bias, argmax, lengths, query_terms, score_grad):
    blocks, size = lax.axis_size("seq"), lax.axis_size("dp")
    z = lax.axis_index("seq")
    tok_rows = hidden.shape[1]
    entries, width = head_weight.shape
    parts = [tok_rows * share // 8 for share in SHARES]
    firsts = [sum(parts[:i]) for i in range(len(parts))]
    count = len(parts)
    even = tuple(range(2, blocks, 2))
    near = even + (1,)
    far = tuple(range(3, blocks, 2))
    bits = [1 << i for i in range(blocks.bit_length() - 1)]

    def swap(x):
        return lax.all_to_all(x, "dp", split_axis=0, concat_axis=0, tiled=True)

    sents = []
    for part, first in zip(parts, firsts):
        sent = hidden[:, first : first + part]
        sents.append(sent.reshape(-1, part, size, width).transpose(2, 0, 1, 3).reshape(-1, part, width))

    held = [dict() for _ in range(count)]
    partials, logits = [None] * count, [None] * count
    grads = [dict() for _ in range(count)]
    clock = []

    def tie(*values):
        out = together(*values, *clock)
        clock[:] = out[len(values) :]
        return out[: len(values)]

    def gather_near(c):
        for bit in reversed(bits):
            for slot in sorted(held[c]) if bit > 1 else (0,):
                held[c][slot ^ bit] = exchange(held[c][slot], "seq", bit)

    def gather_far(c):
        for slot in far:
            held[c][slot] = exchange(held[c][slot ^ 1], "seq", 1)

    def run_forward(c, slots, *others):
        sources = [held[c][slot] for slot in slots]
        waits = tuple(clock) + others
        join = (pooled,) if c == 0 and slots == far else ()
        partials[c] = forward(codes[c], weights_t, slots, sources, partials[c], join, waits)
        clock[:] = [partials[c]]

    def run_backward(c, slots, *others):
        waits = tuple(clock) + others
        found = backward(
            codes[c], head_weight, logits[c], logits[0], bias, slots, parts[c], waits
        )
        grads[c].update(zip(slots, found))
        clock[:] = [found[0]]

    def reduce_far(c):
        for slot in reversed(far):
            grads[c][slot] = exchange(grads[c][slot].astype(BF16), "seq", 1)

    def reduce_near(c):
        grads[c][1] = exchange(grads[c][1].astype(BF16), "seq", 1)
        for slot in far:
            grads[c][slot ^ 1] = grads[c][slot ^ 1] + grads[c].pop(slot).astype(F32)
        for bit in bits[1:]:
            for slot in range(blocks - bit, 0, -2 * bit):
                moved = exchange(grads[c].pop(slot).astype(BF16), "seq", bit)
                if slot == bit:
                    grads[c][slot] = moved
                else:
                    grads[c][slot ^ bit] = grads[c][slot ^ bit] + moved.astype(F32)

    def run_sum(value, *between, start=1):
        step = start
        while step < size:
            value = value + exchange(value, "dp", step)
            if between:
                between[0](value)
                between = between[1:]
            step *= 2
        return value

    held[0][0] = swap(sents[0])
    gather_near(0)

    head_weight, saved_all, queries, scores, held[0][0] = together(
        head_weight, argmax, query_terms, score_grad, held[0][0]
    )
    saved = lax.dynamic_slice_in_dim(saved_all, z * entries, entries, 1)
    block = saved // tok_rows
    inner = saved - block * tok_rows
    kept = (block < blocks) & (saved < lengths[:, None])
    codes = []
    for part, first in zip(parts, firsts):
        here = kept & (inner >= first) & (inner < first + part)
        codes.append(jnp.where(here, (block ^ z) * part + inner - first, -1))
    sents[1:], codes = together(sents[1:], codes)
    bias = head_bias.astype(F32)[None, :]
    queries = lax.dynamic_slice_in_dim(queries, z * entries, entries, 1)
    pooled = jnp.einsum("jd,jv->dv", scores, queries, preferred_element_type=F32)
    weights_t = head_weight.T
    run_forward(0, (0,))
    for c in range(1, count):
        held[c][0] = swap(sents[c])
    arrived = [held[0][slot] for slot in near]
    arrived = tie(*arrived, *[held[c][0] for c in range(1, count)])
    held[0].update(zip(near, arrived))
    for c in range(1, count):
        held[c][0] = arrived[len(near) + c - 1]
    gather_far(0)

    for c in range(1, count + 1):
        more = c < count
        if more:
            gather_near(c)
        run_forward(c - 1, near)
        run_forward(c - 1, far)
        between = []
        if more:
            between.append(lambda value: run_forward(c, (0,), value))
        elif count > 1:
            between.append(lambda value: run_backward(c - 2, (0,), value))
        value = partials[c - 1]
        if c > 1:
            value = value + exchange(value, "dp", 1)
            value, *got = together(value, *[grads[c - 2][slot] for slot in far])
            grads[c - 2].update(zip(far, got))
            reduce_near(c - 2)
            logits[c - 1] = run_sum(value, *between, start=2)
        else:
            logits[c - 1] = run_sum(value, *between)
        if more:
            arrived = tie(*[held[c][slot] for slot in near])
            held[c].update(zip(near, arrived))
            gather_far(c)
        run_backward(c - 1, far)
        reduce_far(c - 1)
        run_backward(c - 1, even, *((grads[c - 2][1],) if c > 1 else ()))
        run_backward(c - 1, (1,), *([grads[c - 2][bit] for bit in bits[1:]] if c > 1 else ()))
    reduce_near(count - 1)
    run_backward(count - 1, (0,))

    results = []
    for c in range(count):
        total = grads[c].pop(0)
        for moved in grads[c].values():
            total = total + moved.astype(F32)
        back = swap(total.astype(BF16))
        back = back.reshape(size, -1, parts[c], width).transpose(1, 2, 0, 3)
        results.append(back.reshape(-1, parts[c], size * width))
    return jnp.concatenate(results, axis=1)


def solution(mesh):
    return jax.shard_map(
        on_device,
        mesh=mesh,
        in_specs=(
            P("dp", "seq", None),
            P("seq", "dp"),
            P("seq"),
            P(),
            P(),
            P("dp", None),
            P("dp", None),
        ),
        out_specs=P("dp", "seq", None),
        check_vma=False,
    )
```

```python
import functools

import jax
import jax.numpy as jnp
from jax import lax
from jax.experimental import pallas as pl
from jax.experimental.pallas import tpu as pltpu
from jax.sharding import PartitionSpec as P

F32, BF16, I32 = jnp.float32, jnp.bfloat16, jnp.int32
SHARES = (4, 4)
VMEM_LIMIT = 28 * 1024 * 1024
TILE = 1024
ANY = pl.BlockSpec(memory_space=pl.ANY)
FAR = pl.BlockSpec(memory_space=pltpu.HBM)
SCALAR = pl.BlockSpec(memory_space=pltpu.SMEM)


def tile_of(total):
    return TILE if total % TILE == 0 else total


def columns(side, k, half):
    at = side[0] if k == 0 else 1 - side[0]
    return pl.ds(pl.multiple_of(at * half, half), half)


def weights_of_step(side, sources, buffer, arrived):
    tile, half = buffer.shape[0] // arrived.shape[1], buffer.shape[1] // 2
    step = pl.program_id(0)

    def copy(k, t):
        where_at = pl.ds(t * tile, tile)
        target = buffer.at[where_at, columns(side, k, half)]
        return pltpu.make_async_copy(sources[k].at[where_at], target, arrived.at[k, t])

    @pl.when(step == 0)
    def _():
        for t in range(arrived.shape[1]):
            for k in range(2):
                copy(k, t).start()

    for k in range(2):
        copy(k, step).wait()
    return buffer[pl.ds(pl.multiple_of(step * tile, tile), tile), :]


def score(rows, weights):
    return lax.dot_general(rows, weights, (((1,), (1,)), ((), ())), preferred_element_type=F32)


def forward_kernel(slots, grows, joined, side, code, mine, other, *rest):
    before, sources = rest[:grows], rest[grows : grows + len(slots)]
    out, buffer, arrived = rest[-3:]
    weights = weights_of_step(side, (mine, other), buffer, arrived)
    codes = code[...]
    total = before[0][...] if grows else jnp.zeros(codes.shape, F32)
    for slot, source in zip(slots, sources):
        docs, part, width = source.shape
        scores = score(source[...].reshape(docs * part, width), weights)
        scores = scores.reshape(docs, part, scores.shape[1])
        ids = lax.broadcasted_iota(I32, scores.shape, 1) + slot * part
        hit = ids == codes[:, None, :]
        total += jnp.sum(jnp.where(hit, scores, 0.0), axis=1)
    if joined:
        out[pl.ds(0, codes.shape[0]), :] = total
        out[pl.ds(codes.shape[0], codes.shape[0]), :] = rest[grows + len(slots)][...]
    else:
        out[...] = total


def backward_kernel(slots, waits, side, code, mine, other, logits, joined, bias, *rest):
    outs, buffer, arrived = rest[waits:-2], rest[-2], rest[-1]
    weights = weights_of_step(side, (mine, other), buffer, arrived)
    step = pl.program_id(0)
    docs = code.shape[0]
    x = logits[pl.ds(0, docs), :] + bias[...]
    soft = jnp.maximum(x, 0.0) + jnp.log1p(jnp.exp(-jnp.abs(x)))
    factor = joined[pl.ds(docs, docs), :] * jax.nn.sigmoid(x) / (1.0 + soft)
    delta = factor.astype(BF16).astype(F32)
    codes = code[...]
    for slot, out in zip(slots, outs):
        docs, part, width = out.shape
        ids = lax.broadcasted_iota(I32, (docs, part, codes.shape[1]), 1) + slot * part
        hit = ids == codes[:, None, :]
        spread = jnp.where(hit, delta[:, None, :], 0.0).astype(BF16)
        spread = spread.reshape(docs * part, codes.shape[1])
        grown = jnp.dot(spread, weights, preferred_element_type=F32)
        grown = grown.reshape(docs, part, width)

        @pl.when(step == 0)
        def _():
            out[...] = grown

        @pl.when(step > 0)
        def _():
            out[...] += grown


def forward(side, code, mine, other, slots, sources, before, join, waits):
    docs, part, width = sources[0].shape
    entries = mine.shape[0]
    tile = tile_of(entries)
    logit = pl.BlockSpec((docs, tile), lambda t: (0, t))
    rows = pl.BlockSpec((docs, part, width), lambda t: (0, 0, 0))
    flops = 2 * docs * part * width * entries * len(slots)
    before = [] if before is None else [before]
    high = docs * (1 + len(join))
    return pl.pallas_call(
        functools.partial(forward_kernel, slots, len(before), len(join)),
        out_shape=jax.ShapeDtypeStruct((high, entries), F32),
        grid=(entries // tile,),
        in_specs=[SCALAR, logit, FAR, FAR]
        + [logit] * len(before)
        + [rows] * len(slots)
        + [logit] * len(join)
        + [ANY] * len(waits),
        out_specs=pl.BlockSpec((high, tile), lambda t: (0, t)),
        scratch_shapes=[
            pltpu.VMEM((entries, width), BF16),
            pltpu.SemaphoreType.DMA((2, entries // tile)),
        ],
        compiler_params=pltpu.CompilerParams(vmem_limit_bytes=VMEM_LIMIT),
        cost_estimate=pl.CostEstimate(flops=flops, bytes_accessed=6 << 20, transcendentals=0),
        name="forward",
    )(side, code, mine, other, *before, *sources, *join, *waits)


def backward(side, code, mine, other, logits, joined, bias, slots, part, waits):
    docs, entries = code.shape
    width = 2 * mine.shape[1]
    tile = tile_of(entries)
    whole = pl.BlockSpec((docs, tile), lambda t: (0, t))
    flops = 2 * docs * part * width * entries * len(slots)
    return pl.pallas_call(
        functools.partial(backward_kernel, slots, len(waits)),
        out_shape=[jax.ShapeDtypeStruct((docs, part, width), F32)] * len(slots),
        grid=(entries // tile,),
        in_specs=[
            SCALAR,
            whole,
            FAR,
            FAR,
            pl.BlockSpec((logits.shape[0], tile), lambda t: (0, t)),
            pl.BlockSpec((2 * docs, tile), lambda t: (0, t)),
            pl.BlockSpec((1, tile), lambda t: (0, t)),
        ]
        + [ANY] * len(waits),
        out_specs=[pl.BlockSpec((docs, part, width), lambda t: (0, 0, 0))] * len(slots),
        scratch_shapes=[
            pltpu.VMEM((entries, width), BF16),
            pltpu.SemaphoreType.DMA((2, entries // tile)),
        ],
        compiler_params=pltpu.CompilerParams(vmem_limit_bytes=VMEM_LIMIT),
        cost_estimate=pl.CostEstimate(flops=flops, bytes_accessed=6 << 20, transcendentals=0),
        name="backward",
    )(side, code, mine, other, logits, joined, bias, *waits)


def together(*values):
    return lax.optimization_barrier(values)


def exchange(value, axis, bit):
    return lax.ppermute(value, axis, [(i, i ^ bit) for i in range(lax.axis_size(axis))])


def on_device(hidden, head_weight, head_bias, argmax, lengths, query_terms, score_grad):
    blocks, size = lax.axis_size("seq"), lax.axis_size("dp")
    z = lax.axis_index("seq")
    core = lax.axis_index("dp") % 2
    side = jnp.reshape(core, (1,)).astype(I32)
    pairs = size // 2
    groups = [list(range(side, size, 2)) for side in (0, 1)]
    tok_rows = hidden.shape[1]
    entries, width = head_weight.shape
    parts = [tok_rows * share // 8 for share in SHARES]
    firsts = [sum(parts[:i]) for i in range(len(parts))]
    count = len(parts)
    even = tuple(range(2, blocks, 2))
    near = even + (1,)
    far = tuple(range(3, blocks, 2))
    bits = [1 << i for i in range(blocks.bit_length() - 1)]

    def swap(x):
        return lax.all_to_all(
            x, "dp", split_axis=0, concat_axis=0, axis_index_groups=groups, tiled=True
        )

    def own_docs(x):
        x = x.reshape((pairs, 2, x.shape[0] // size) + x.shape[1:])
        x = lax.dynamic_index_in_dim(x, core, 1, keepdims=False)
        return x.reshape((-1,) + x.shape[2:])

    sents = []
    for part, first in zip(parts, firsts):
        sent = hidden[:, first : first + part]
        sent = sent.reshape(-1, part, pairs, 2 * width).transpose(2, 0, 1, 3)
        sents.append(sent.reshape(-1, part, 2 * width))

    held = [dict() for _ in range(count)]
    partials, logits = [None] * count, [None] * count
    grads = [dict() for _ in range(count)]
    clock = []

    def tie(*values):
        out = together(*values, *clock)
        clock[:] = out[len(values) :]
        return out[: len(values)]

    def gather_near(c):
        for bit in reversed(bits):
            for slot in sorted(held[c]) if bit > 1 else (0,):
                held[c][slot ^ bit] = exchange(held[c][slot], "seq", bit)

    def gather_far(c):
        for slot in far:
            held[c][slot] = exchange(held[c][slot ^ 1], "seq", 1)

    def run_forward(c, slots, *others):
        sources = [held[c][slot] for slot in slots]
        waits = tuple(clock) + others
        join = (pooled,) if c == 0 and slots == far else ()
        partials[c] = forward(side, codes[c], mine, other, slots, sources, partials[c], join, waits)
        clock[:] = [partials[c]]

    def run_backward(c, slots, *others):
        waits = tuple(clock) + others
        found = backward(
            side, codes[c], mine, other, logits[c], logits[0], bias, slots, parts[c], waits
        )
        grads[c].update(zip(slots, found))
        clock[:] = [found[0]]

    def reduce_far(c):
        for slot in reversed(far):
            grads[c][slot] = exchange(grads[c][slot].astype(BF16), "seq", 1)

    def reduce_near(c):
        grads[c][1] = exchange(grads[c][1].astype(BF16), "seq", 1)
        for slot in far:
            grads[c][slot ^ 1] = grads[c][slot ^ 1] + grads[c].pop(slot).astype(F32)
        for bit in bits[1:]:
            for slot in range(blocks - bit, 0, -2 * bit):
                moved = exchange(grads[c].pop(slot).astype(BF16), "seq", bit)
                if slot == bit:
                    grads[c][slot] = moved
                else:
                    grads[c][slot ^ bit] = grads[c][slot ^ bit] + moved.astype(F32)

    def run_sum(value, *between, start=2):
        step = start
        while step < size:
            value = value + exchange(value, "dp", step)
            if between:
                between[0](value)
                between = between[1:]
            step *= 2
        return value

    other = exchange(head_weight, "dp", 1)
    held[0][0] = swap(sents[0])
    gather_near(0)

    mine, saved_all, queries, scores, held[0][0] = together(
        head_weight, argmax, query_terms, score_grad, held[0][0]
    )
    saved = own_docs(lax.dynamic_slice_in_dim(saved_all, z * entries, entries, 1))
    block = saved // tok_rows
    inner = saved - block * tok_rows
    kept = (block < blocks) & (saved < own_docs(lengths)[:, None])
    codes = []
    for part, first in zip(parts, firsts):
        here = kept & (inner >= first) & (inner < first + part)
        codes.append(jnp.where(here, (block ^ z) * part + inner - first, -1))
    bias = head_bias.astype(F32)[None, :]
    queries = lax.dynamic_slice_in_dim(queries, z * entries, entries, 1)
    pooled = jnp.einsum("jd,jv->dv", scores, queries, preferred_element_type=F32)
    pooled = pooled.reshape((pairs, 2, -1, entries))
    kept_part = lax.dynamic_index_in_dim(pooled, core, 1, keepdims=False)
    sent_part = lax.dynamic_index_in_dim(pooled, 1 - core, 1, keepdims=False)
    pooled = (kept_part + exchange(sent_part, "dp", 1)).reshape(-1, entries)
    run_forward(0, (0,))
    sents[1:] = tie(*sents[1:])
    for c in range(1, count):
        held[c][0] = swap(sents[c])
    arrived = [held[0][slot] for slot in near]
    arrived = tie(*arrived, *[held[c][0] for c in range(1, count)])
    held[0].update(zip(near, arrived))
    for c in range(1, count):
        held[c][0] = arrived[len(near) + c - 1]
    gather_far(0)

    for c in range(1, count + 1):
        more = c < count
        if more:
            gather_near(c)
        if c == 1:
            run_forward(0, near)
        run_forward(c - 1, far)
        value = partials[c - 1]
        if c > 1:
            value = value + exchange(value, "dp", 2)
            value, *got = together(value, *[grads[c - 2][slot] for slot in far])
            grads[c - 2].update(zip(far, got))
            reduce_near(c - 2)
            logits[c - 1] = run_sum(value, start=4)
        else:
            logits[c - 1] = run_sum(value)
        run_backward(c - 1, far)
        reduce_far(c - 1)
        if more:
            arrived = tie(*[held[c][slot] for slot in near])
            held[c].update(zip(near, arrived))
            gather_far(c)
            run_forward(c, (0,) + near)
            run_backward(c - 1, near)
        else:
            run_backward(c - 1, even, *((grads[c - 2][1],) if c > 1 else ()))
            run_backward(c - 1, (1,), *([grads[c - 2][bit] for bit in bits[1:]] if c > 1 else ()))
    reduce_near(count - 1)
    for c in range(count):
        run_backward(c, (0,))

    results = []
    for c in range(count):
        total = grads[c].pop(0)
        for moved in grads[c].values():
            total = total + moved.astype(F32)
        back = swap(total.astype(BF16))
        back = back.reshape(pairs, -1, parts[c], 2 * width).transpose(1, 2, 0, 3)
        results.append(back.reshape(-1, parts[c], size * width))
    return jnp.concatenate(results, axis=1)


def solution(mesh):
    return jax.shard_map(
        on_device,
        mesh=mesh,
        in_specs=(
            P("dp", "seq", None),
            P("seq", "dp"),
            P("seq"),
            P(),
            P(),
            P("dp", None),
            P("dp", None),
        ),
        out_specs=P("dp", "seq", None),
        check_vma=False,
    )
```

```python
import functools

import jax
import jax.numpy as jnp
from jax import lax
from jax.experimental import pallas as pl
from jax.experimental.pallas import tpu as pltpu
from jax.sharding import PartitionSpec as P

F32, BF16, I32 = jnp.float32, jnp.bfloat16, jnp.int32
SHARES = (4, 4)
VMEM_LIMIT = 28 * 1024 * 1024
TILE = 1024
ANY = pl.BlockSpec(memory_space=pl.ANY)
FAR = pl.BlockSpec(memory_space=pltpu.HBM)
SCALAR = pl.BlockSpec(memory_space=pltpu.SMEM)


def tile_of(total):
    return TILE if total % TILE == 0 else total


def columns(side, k, half):
    at = side[0] if k == 0 else 1 - side[0]
    return pl.ds(pl.multiple_of(at * half, half), half)


def weights_of_step(side, sources, buffer, arrived):
    tile, half = buffer.shape[0] // arrived.shape[1], buffer.shape[1] // 2
    step = pl.program_id(0)

    def copy(k, t):
        where_at = pl.ds(t * tile, tile)
        target = buffer.at[where_at, columns(side, k, half)]
        return pltpu.make_async_copy(sources[k].at[where_at], target, arrived.at[k, t])

    @pl.when(step == 0)
    def _():
        for t in range(arrived.shape[1]):
            for k in range(2):
                copy(k, t).start()

    for k in range(2):
        copy(k, step).wait()
    return buffer[pl.ds(pl.multiple_of(step * tile, tile), tile), :]


def score(rows, weights):
    return lax.dot_general(rows, weights, (((1,), (1,)), ((), ())), preferred_element_type=F32)


def forward_kernel(slots, grows, joined, side, code, mine, other, *rest):
    before, sources = rest[:grows], rest[grows : grows + len(slots)]
    out, buffer, arrived = rest[-3:]
    weights = weights_of_step(side, (mine, other), buffer, arrived)
    codes = code[...]
    total = before[0][...] if grows else jnp.zeros(codes.shape, F32)
    for slot, source in zip(slots, sources):
        docs, part, width = source.shape
        scores = score(source[...].reshape(docs * part, width), weights)
        scores = scores.reshape(docs, part, scores.shape[1])
        ids = lax.broadcasted_iota(I32, scores.shape, 1) + slot * part
        hit = ids == codes[:, None, :]
        total += jnp.sum(jnp.where(hit, scores, 0.0), axis=1)
    if joined:
        out[pl.ds(0, codes.shape[0]), :] = total
        out[pl.ds(codes.shape[0], codes.shape[0]), :] = rest[grows + len(slots)][...]
    else:
        out[...] = total


def backward_kernel(slots, waits, side, code, mine, other, logits, joined, bias, *rest):
    outs, buffer, arrived = rest[waits:-2], rest[-2], rest[-1]
    weights = weights_of_step(side, (mine, other), buffer, arrived)
    step = pl.program_id(0)
    docs = code.shape[0]
    x = logits[pl.ds(0, docs), :] + bias[...]
    soft = jnp.maximum(x, 0.0) + jnp.log1p(jnp.exp(-jnp.abs(x)))
    factor = joined[pl.ds(docs, docs), :] * jax.nn.sigmoid(x) / (1.0 + soft)
    delta = factor.astype(BF16).astype(F32)
    codes = code[...]
    for slot, out in zip(slots, outs):
        docs, part, width = out.shape
        ids = lax.broadcasted_iota(I32, (docs, part, codes.shape[1]), 1) + slot * part
        hit = ids == codes[:, None, :]
        spread = jnp.where(hit, delta[:, None, :], 0.0).astype(BF16)
        spread = spread.reshape(docs * part, codes.shape[1])
        grown = jnp.dot(spread, weights, preferred_element_type=F32)
        grown = grown.reshape(docs, part, width)

        @pl.when(step == 0)
        def _():
            out[...] = grown

        @pl.when(step > 0)
        def _():
            out[...] += grown


def forward(side, code, mine, other, slots, sources, before, join, waits):
    docs, part, width = sources[0].shape
    entries = mine.shape[0]
    tile = tile_of(entries)
    logit = pl.BlockSpec((docs, tile), lambda t: (0, t))
    rows = pl.BlockSpec((docs, part, width), lambda t: (0, 0, 0))
    flops = 2 * docs * part * width * entries * len(slots)
    before = [] if before is None else [before]
    high = docs * (1 + len(join))
    return pl.pallas_call(
        functools.partial(forward_kernel, slots, len(before), len(join)),
        out_shape=jax.ShapeDtypeStruct((high, entries), F32),
        grid=(entries // tile,),
        in_specs=[SCALAR, logit, FAR, FAR]
        + [logit] * len(before)
        + [rows] * len(slots)
        + [logit] * len(join)
        + [ANY] * len(waits),
        out_specs=pl.BlockSpec((high, tile), lambda t: (0, t)),
        scratch_shapes=[
            pltpu.VMEM((entries, width), BF16),
            pltpu.SemaphoreType.DMA((2, entries // tile)),
        ],
        compiler_params=pltpu.CompilerParams(vmem_limit_bytes=VMEM_LIMIT),
        cost_estimate=pl.CostEstimate(flops=flops, bytes_accessed=6 << 20, transcendentals=0),
        name="forward",
    )(side, code, mine, other, *before, *sources, *join, *waits)


def backward(side, code, mine, other, logits, joined, bias, slots, part, waits):
    docs, entries = code.shape
    width = 2 * mine.shape[1]
    tile = tile_of(entries)
    whole = pl.BlockSpec((docs, tile), lambda t: (0, t))
    flops = 2 * docs * part * width * entries * len(slots)
    return pl.pallas_call(
        functools.partial(backward_kernel, slots, len(waits)),
        out_shape=[jax.ShapeDtypeStruct((docs, part, width), F32)] * len(slots),
        grid=(entries // tile,),
        in_specs=[
            SCALAR,
            whole,
            FAR,
            FAR,
            pl.BlockSpec((logits.shape[0], tile), lambda t: (0, t)),
            pl.BlockSpec((2 * docs, tile), lambda t: (0, t)),
            pl.BlockSpec((1, tile), lambda t: (0, t)),
        ]
        + [ANY] * len(waits),
        out_specs=[pl.BlockSpec((docs, part, width), lambda t: (0, 0, 0))] * len(slots),
        scratch_shapes=[
            pltpu.VMEM((entries, width), BF16),
            pltpu.SemaphoreType.DMA((2, entries // tile)),
        ],
        compiler_params=pltpu.CompilerParams(vmem_limit_bytes=VMEM_LIMIT),
        cost_estimate=pl.CostEstimate(flops=flops, bytes_accessed=6 << 20, transcendentals=0),
        name="backward",
    )(side, code, mine, other, logits, joined, bias, *waits)


def together(*values):
    return lax.optimization_barrier(values)


def exchange(value, axis, bit):
    return lax.ppermute(value, axis, [(i, i ^ bit) for i in range(lax.axis_size(axis))])


def on_device(hidden, head_weight, head_bias, argmax, lengths, query_terms, score_grad):
    blocks, size = lax.axis_size("seq"), lax.axis_size("dp")
    z = lax.axis_index("seq")
    core = lax.axis_index("dp") % 2
    side = jnp.reshape(core, (1,)).astype(I32)
    pairs = size // 2
    groups = [list(range(side, size, 2)) for side in (0, 1)]
    tok_rows = hidden.shape[1]
    entries, width = head_weight.shape
    parts = [tok_rows * share // 8 for share in SHARES]
    firsts = [sum(parts[:i]) for i in range(len(parts))]
    count = len(parts)
    even = tuple(range(2, blocks, 2))
    near = even + (1,)
    far = tuple(range(3, blocks, 2))
    bits = [1 << i for i in range(blocks.bit_length() - 1)]

    def swap(x):
        return lax.all_to_all(
            x, "dp", split_axis=0, concat_axis=0, axis_index_groups=groups, tiled=True
        )

    def own_docs(x):
        x = x.reshape((pairs, 2, x.shape[0] // size) + x.shape[1:])
        x = lax.dynamic_index_in_dim(x, core, 1, keepdims=False)
        return x.reshape((-1,) + x.shape[2:])

    sents = []
    for part, first in zip(parts, firsts):
        sent = hidden[:, first : first + part]
        sent = sent.reshape(-1, part, pairs, 2 * width).transpose(2, 0, 1, 3)
        sents.append(sent.reshape(-1, part, 2 * width))

    held = [dict() for _ in range(count)]
    partials, logits = [None] * count, [None] * count
    grads = [dict() for _ in range(count)]
    clock = []

    def tie(*values):
        out = together(*values, *clock)
        clock[:] = out[len(values) :]
        return out[: len(values)]

    def gather_near(c):
        for bit in reversed(bits):
            for slot in sorted(held[c]) if bit > 1 else (0,):
                held[c][slot ^ bit] = exchange(held[c][slot], "seq", bit)

    def gather_far(c):
        for slot in far:
            held[c][slot] = exchange(held[c][slot ^ 1], "seq", 1)

    def run_forward(c, slots, *others):
        sources = [held[c][slot] for slot in slots]
        waits = tuple(clock) + others
        join = (pooled,) if c == 0 and slots == far else ()
        partials[c] = forward(side, codes[c], mine, other, slots, sources, partials[c], join, waits)
        clock[:] = [partials[c]]

    def run_backward(c, slots, *others):
        waits = tuple(clock) + others
        found = backward(
            side, codes[c], mine, other, logits[c], logits[0], bias, slots, parts[c], waits
        )
        grads[c].update(zip(slots, found))
        clock[:] = [found[0]]

    def reduce_far(c):
        for slot in reversed(far):
            grads[c][slot] = exchange(grads[c][slot].astype(BF16), "seq", 1)

    def reduce_near(c):
        grads[c][1] = exchange(grads[c][1].astype(BF16), "seq", 1)
        for slot in far:
            grads[c][slot ^ 1] = grads[c][slot ^ 1] + grads[c].pop(slot).astype(F32)
        for bit in bits[1:]:
            for slot in range(blocks - bit, 0, -2 * bit):
                moved = exchange(grads[c].pop(slot).astype(BF16), "seq", bit)
                if slot == bit:
                    grads[c][slot] = moved
                else:
                    grads[c][slot ^ bit] = grads[c][slot ^ bit] + moved.astype(F32)

    def run_sum(value, *between, start=2):
        step = start
        while step < size:
            value = value + exchange(value, "dp", step)
            if between:
                between[0](value)
                between = between[1:]
            step *= 2
        return value

    other = exchange(head_weight, "dp", 1)
    held[0][0] = swap(sents[0])
    gather_near(0)

    mine, saved_all, queries, scores, held[0][0] = together(
        head_weight, argmax, query_terms, score_grad, held[0][0]
    )
    saved = own_docs(lax.dynamic_slice_in_dim(saved_all, z * entries, entries, 1))
    block = saved // tok_rows
    inner = saved - block * tok_rows
    kept = (block < blocks) & (saved < own_docs(lengths)[:, None])
    codes = []
    for part, first in zip(parts, firsts):
        here = kept & (inner >= first) & (inner < first + part)
        codes.append(jnp.where(here, (block ^ z) * part + inner - first, -1))
    bias = head_bias.astype(F32)[None, :]
    queries = lax.dynamic_slice_in_dim(queries, z * entries, entries, 1)
    pooled = jnp.einsum("jd,jv->dv", scores, queries, preferred_element_type=F32)
    pooled = pooled.reshape((pairs, 2, -1, entries))
    kept_part = lax.dynamic_index_in_dim(pooled, core, 1, keepdims=False)
    sent_part = lax.dynamic_index_in_dim(pooled, 1 - core, 1, keepdims=False)
    pooled = (kept_part + exchange(sent_part, "dp", 1)).reshape(-1, entries)
    run_forward(0, (0,))
    sents[1:] = tie(*sents[1:])
    for c in range(1, count):
        held[c][0] = swap(sents[c])
    arrived = [held[0][slot] for slot in near]
    arrived = tie(*arrived, *[held[c][0] for c in range(1, count)])
    held[0].update(zip(near, arrived))
    for c in range(1, count):
        held[c][0] = arrived[len(near) + c - 1]
    gather_far(0)

    for c in range(1, count + 1):
        more = c < count
        if more:
            gather_near(c)
        if c == 1:
            run_forward(0, near)
        run_forward(c - 1, far)
        value = partials[c - 1]
        if c > 1:
            value = value + exchange(value, "dp", 2)
            value, *got = together(value, *[grads[c - 2][slot] for slot in far])
            grads[c - 2].update(zip(far, got))
            reduce_near(c - 2)
            logits[c - 1] = run_sum(value, start=4)
        else:
            logits[c - 1] = run_sum(value)
        run_backward(c - 1, far)
        reduce_far(c - 1)
        if more:
            arrived = together(*[held[c][slot] for slot in near])
            held[c].update(zip(near, arrived))
            gather_far(c)
            run_forward(c, (0,) + near)
            run_backward(c - 1, near)
        else:
            run_backward(c - 1, even, *((grads[c - 2][1],) if c > 1 else ()))
            run_backward(c - 1, (1,), *([grads[c - 2][bit] for bit in bits[1:]] if c > 1 else ()))
    reduce_near(count - 1)
    for c in range(count):
        run_backward(c, (0,))

    results = []
    for c in range(count):
        total = grads[c].pop(0)
        for moved in grads[c].values():
            total = total + moved.astype(F32)
        back = swap(total.astype(BF16))
        back = back.reshape(pairs, -1, parts[c], 2 * width).transpose(1, 2, 0, 3)
        results.append(back.reshape(-1, parts[c], size * width))
    return jnp.concatenate(results, axis=1)


def solution(mesh):
    return jax.shard_map(
        on_device,
        mesh=mesh,
        in_specs=(
            P("dp", "seq", None),
            P("seq", "dp"),
            P("seq"),
            P(),
            P(),
            P("dp", None),
            P("dp", None),
        ),
        out_specs=P("dp", "seq", None),
        check_vma=False,
    )
```

```python
import functools

import jax
import jax.numpy as jnp
from jax import lax
from jax.experimental import pallas as pl
from jax.experimental.pallas import tpu as pltpu
from jax.sharding import PartitionSpec as P

F32, BF16, I32 = jnp.float32, jnp.bfloat16, jnp.int32
SHARES = (4, 4)
VMEM_LIMIT = 28 * 1024 * 1024
TILE = 1024
ANY = pl.BlockSpec(memory_space=pl.ANY)
FAR = pl.BlockSpec(memory_space=pltpu.HBM)
SCALAR = pl.BlockSpec(memory_space=pltpu.SMEM)


def tile_of(total):
    return TILE if total % TILE == 0 else total


def columns(side, k, half):
    at = side[0] if k == 0 else 1 - side[0]
    return pl.ds(pl.multiple_of(at * half, half), half)


def weights_of_step(side, sources, buffer, arrived):
    tile, half = buffer.shape[0] // arrived.shape[1], buffer.shape[1] // 2
    step = pl.program_id(0)

    def copy(k, t):
        where_at = pl.ds(t * tile, tile)
        target = buffer.at[where_at, columns(side, k, half)]
        return pltpu.make_async_copy(sources[k].at[where_at], target, arrived.at[k, t])

    @pl.when(step == 0)
    def _():
        for t in range(arrived.shape[1]):
            for k in range(2):
                copy(k, t).start()

    for k in range(2):
        copy(k, step).wait()
    return buffer[pl.ds(pl.multiple_of(step * tile, tile), tile), :]


def score(rows, weights):
    return lax.dot_general(rows, weights, (((1,), (1,)), ((), ())), preferred_element_type=F32)


def forward_kernel(slots, grows, joined, side, code, mine, other, *rest):
    before, sources = rest[:grows], rest[grows : grows + len(slots)]
    out, buffer, arrived = rest[-3:]
    weights = weights_of_step(side, (mine, other), buffer, arrived)
    codes = code[...]
    total = before[0][...] if grows else jnp.zeros(codes.shape, F32)
    for slot, source in zip(slots, sources):
        docs, part, width = source.shape
        scores = score(source[...].reshape(docs * part, width), weights)
        scores = scores.reshape(docs, part, scores.shape[1])
        ids = lax.broadcasted_iota(I32, scores.shape, 1) + slot * part
        hit = ids == codes[:, None, :]
        total += jnp.sum(jnp.where(hit, scores, 0.0), axis=1)
    if joined:
        out[pl.ds(0, codes.shape[0]), :] = total
        out[pl.ds(codes.shape[0], codes.shape[0]), :] = rest[grows + len(slots)][...]
    else:
        out[...] = total


def backward_kernel(slots, waits, side, code, mine, other, logits, joined, bias, *rest):
    outs, buffer, arrived = rest[waits:-2], rest[-2], rest[-1]
    weights = weights_of_step(side, (mine, other), buffer, arrived)
    step = pl.program_id(0)
    docs = code.shape[0]
    x = logits[pl.ds(0, docs), :] + bias[...]
    soft = jnp.maximum(x, 0.0) + jnp.log1p(jnp.exp(-jnp.abs(x)))
    factor = joined[pl.ds(docs, docs), :] * jax.nn.sigmoid(x) / (1.0 + soft)
    delta = factor.astype(BF16).astype(F32)
    codes = code[...]
    for slot, out in zip(slots, outs):
        docs, part, width = out.shape
        ids = lax.broadcasted_iota(I32, (docs, part, codes.shape[1]), 1) + slot * part
        hit = ids == codes[:, None, :]
        spread = jnp.where(hit, delta[:, None, :], 0.0).astype(BF16)
        spread = spread.reshape(docs * part, codes.shape[1])
        grown = jnp.dot(spread, weights, preferred_element_type=F32)
        grown = grown.reshape(docs, part, width)

        @pl.when(step == 0)
        def _():
            out[...] = grown

        @pl.when(step > 0)
        def _():
            out[...] += grown


def forward(side, code, mine, other, slots, sources, before, join, waits):
    docs, part, width = sources[0].shape
    entries = mine.shape[0]
    tile = tile_of(entries)
    logit = pl.BlockSpec((docs, tile), lambda t: (0, t))
    rows = pl.BlockSpec((docs, part, width), lambda t: (0, 0, 0))
    flops = 2 * docs * part * width * entries * len(slots)
    before = [] if before is None else [before]
    high = docs * (1 + len(join))
    return pl.pallas_call(
        functools.partial(forward_kernel, slots, len(before), len(join)),
        out_shape=jax.ShapeDtypeStruct((high, entries), F32),
        grid=(entries // tile,),
        in_specs=[SCALAR, logit, FAR, FAR]
        + [logit] * len(before)
        + [rows] * len(slots)
        + [logit] * len(join)
        + [ANY] * len(waits),
        out_specs=pl.BlockSpec((high, tile), lambda t: (0, t)),
        scratch_shapes=[
            pltpu.VMEM((entries, width), BF16),
            pltpu.SemaphoreType.DMA((2, entries // tile)),
        ],
        compiler_params=pltpu.CompilerParams(vmem_limit_bytes=VMEM_LIMIT),
        cost_estimate=pl.CostEstimate(flops=flops, bytes_accessed=6 << 20, transcendentals=0),
        name="forward",
    )(side, code, mine, other, *before, *sources, *join, *waits)


def backward(side, code, mine, other, logits, joined, bias, slots, part, waits):
    docs, entries = code.shape
    width = 2 * mine.shape[1]
    tile = tile_of(entries)
    whole = pl.BlockSpec((docs, tile), lambda t: (0, t))
    flops = 2 * docs * part * width * entries * len(slots)
    return pl.pallas_call(
        functools.partial(backward_kernel, slots, len(waits)),
        out_shape=[jax.ShapeDtypeStruct((docs, part, width), F32)] * len(slots),
        grid=(entries // tile,),
        in_specs=[
            SCALAR,
            whole,
            FAR,
            FAR,
            pl.BlockSpec((logits.shape[0], tile), lambda t: (0, t)),
            pl.BlockSpec((2 * docs, tile), lambda t: (0, t)),
            pl.BlockSpec((1, tile), lambda t: (0, t)),
        ]
        + [ANY] * len(waits),
        out_specs=[pl.BlockSpec((docs, part, width), lambda t: (0, 0, 0))] * len(slots),
        scratch_shapes=[
            pltpu.VMEM((entries, width), BF16),
            pltpu.SemaphoreType.DMA((2, entries // tile)),
        ],
        compiler_params=pltpu.CompilerParams(vmem_limit_bytes=VMEM_LIMIT),
        cost_estimate=pl.CostEstimate(flops=flops, bytes_accessed=6 << 20, transcendentals=0),
        name="backward",
    )(side, code, mine, other, logits, joined, bias, *waits)


def together(*values):
    return lax.optimization_barrier(values)


def exchange(value, axis, bit):
    return lax.ppermute(value, axis, [(i, i ^ bit) for i in range(lax.axis_size(axis))])


def on_device(hidden, head_weight, head_bias, argmax, lengths, query_terms, score_grad):
    blocks, size = lax.axis_size("seq"), lax.axis_size("dp")
    z = lax.axis_index("seq")
    core = lax.axis_index("dp") % 2
    side = jnp.reshape(core, (1,)).astype(I32)
    pairs = size // 2
    groups = [list(range(side, size, 2)) for side in (0, 1)]
    tok_rows = hidden.shape[1]
    entries, width = head_weight.shape
    parts = [tok_rows * share // 8 for share in SHARES]
    firsts = [sum(parts[:i]) for i in range(len(parts))]
    count = len(parts)
    even = tuple(range(2, blocks, 2))
    near = even + (1,)
    far = tuple(range(3, blocks, 2))
    bits = [1 << i for i in range(blocks.bit_length() - 1)]

    def swap(x):
        return lax.all_to_all(
            x, "dp", split_axis=0, concat_axis=0, axis_index_groups=groups, tiled=True
        )

    def own_docs(x):
        x = x.reshape((pairs, 2, x.shape[0] // size) + x.shape[1:])
        x = lax.dynamic_index_in_dim(x, core, 1, keepdims=False)
        return x.reshape((-1,) + x.shape[2:])

    sents = []
    for part, first in zip(parts, firsts):
        sent = hidden[:, first : first + part]
        sent = sent.reshape(-1, part, pairs, 2 * width).transpose(2, 0, 1, 3)
        sents.append(sent.reshape(-1, part, 2 * width))

    held = [dict() for _ in range(count)]
    partials, logits = [None] * count, [None] * count
    grads = [dict() for _ in range(count)]
    clock = []

    def tie(*values):
        out = together(*values, *clock)
        clock[:] = out[len(values) :]
        return out[: len(values)]

    def gather_near(c):
        for bit in reversed(bits):
            for slot in sorted(held[c]) if bit > 1 else (0,):
                held[c][slot ^ bit] = exchange(held[c][slot], "seq", bit)

    def gather_far(c):
        for slot in far:
            held[c][slot] = exchange(held[c][slot ^ 1], "seq", 1)

    def run_forward(c, slots, *others):
        sources = [held[c][slot] for slot in slots]
        waits = tuple(clock) + others
        join = (pooled,) if c == 0 and slots == far else ()
        partials[c] = forward(side, codes[c], mine, other, slots, sources, partials[c], join, waits)
        clock[:] = [partials[c]]

    def run_backward(c, slots, *others):
        waits = tuple(clock) + others
        found = backward(
            side, codes[c], mine, other, logits[c], logits[0], bias, slots, parts[c], waits
        )
        grads[c].update(zip(slots, found))
        clock[:] = [found[0]]

    def reduce_far(c):
        for slot in reversed(far):
            grads[c][slot] = exchange(grads[c][slot].astype(BF16), "seq", 1)

    def reduce_near(c):
        grads[c][1] = exchange(grads[c][1].astype(BF16), "seq", 1)
        for slot in far:
            grads[c][slot ^ 1] = grads[c][slot ^ 1] + grads[c].pop(slot).astype(F32)
        for bit in bits[1:]:
            for slot in range(blocks - bit, 0, -2 * bit):
                moved = exchange(grads[c].pop(slot).astype(BF16), "seq", bit)
                if slot == bit:
                    grads[c][slot] = moved
                else:
                    grads[c][slot ^ bit] = grads[c][slot ^ bit] + moved.astype(F32)

    def run_sum(value, *between, start=2):
        step = start
        while step < size:
            value = value + exchange(value, "dp", step)
            if between:
                between[0](value)
                between = between[1:]
            step *= 2
        return value

    other = exchange(head_weight, "dp", 1)
    held[0][0] = swap(sents[0])
    gather_near(0)

    mine, saved_all, queries, scores, held[0][0] = together(
        head_weight, argmax, query_terms, score_grad, held[0][0]
    )
    saved = own_docs(lax.dynamic_slice_in_dim(saved_all, z * entries, entries, 1))
    block = saved // tok_rows
    inner = saved - block * tok_rows
    kept = (block < blocks) & (saved < own_docs(lengths)[:, None])
    codes = []
    for part, first in zip(parts, firsts):
        here = kept & (inner >= first) & (inner < first + part)
        codes.append(jnp.where(here, (block ^ z) * part + inner - first, -1))
    bias = head_bias.astype(F32)[None, :]
    queries = lax.dynamic_slice_in_dim(queries, z * entries, entries, 1)
    pooled = jnp.einsum("jd,jv->dv", scores, queries, preferred_element_type=F32)
    pooled = pooled.reshape((pairs, 2, -1, entries))
    kept_part = lax.dynamic_index_in_dim(pooled, core, 1, keepdims=False)
    sent_part = lax.dynamic_index_in_dim(pooled, 1 - core, 1, keepdims=False)
    pooled = (kept_part + exchange(sent_part, "dp", 1)).reshape(-1, entries)
    run_forward(0, (0,))
    sents[1:] = tie(*sents[1:])
    for c in range(1, count):
        held[c][0] = swap(sents[c])
    arrived = [held[0][slot] for slot in near]
    arrived = tie(*arrived, *[held[c][0] for c in range(1, count)])
    held[0].update(zip(near, arrived))
    for c in range(1, count):
        held[c][0] = arrived[len(near) + c - 1]
    gather_far(0)

    for c in range(1, count + 1):
        more = c < count
        if more:
            gather_near(c)
        if c == 1:
            run_forward(0, near)
        run_forward(c - 1, far)
        value = partials[c - 1]
        if c > 1:
            value = value + exchange(value, "dp", 2)
            value, *got = together(value, *[grads[c - 2][slot] for slot in far])
            grads[c - 2].update(zip(far, got))
            reduce_near(c - 2)
            logits[c - 1] = run_sum(value, start=4)
        else:
            logits[c - 1] = run_sum(value)
        run_backward(c - 1, far, *([grads[c - 2][1]] if c > 1 else ()))
        reduce_far(c - 1)
        if more:
            arrived = together(*[held[c][slot] for slot in near])
            held[c].update(zip(near, arrived))
            gather_far(c)
            run_forward(c, (0,) + near)
            run_backward(c - 1, near)
        else:
            run_backward(c - 1, even)
            run_backward(c - 1, (1,), *([grads[c - 2][bit] for bit in bits[1:]] if c > 1 else ()))
    reduce_near(count - 1)
    for c in range(count):
        run_backward(c, (0,))

    results = []
    for c in range(count):
        total = grads[c].pop(0)
        for moved in grads[c].values():
            total = total + moved.astype(F32)
        back = swap(total.astype(BF16))
        back = back.reshape(pairs, -1, parts[c], 2 * width).transpose(1, 2, 0, 3)
        results.append(back.reshape(-1, parts[c], size * width))
    return jnp.concatenate(results, axis=1)


def solution(mesh):
    return jax.shard_map(
        on_device,
        mesh=mesh,
        in_specs=(
            P("dp", "seq", None),
            P("seq", "dp"),
            P("seq"),
            P(),
            P(),
            P("dp", None),
            P("dp", None),
        ),
        out_specs=P("dp", "seq", None),
        check_vma=False,
    )
```
